32 devices in a mesh: groups: 2 (over x), dev: 8 (over z, y), sub: 2 (over core).
Axes of the slice: x: 2, y: 2, z: 4, core: 2. Of those that a mesh axis runs over, the one named last changes fastest.
Arguments:
- tokens: bfloat16 [4096, 7168], P(('groups', 'dev', 'sub')), parts along dimension 0, may hold values from -6 to 6
- expert_ids: int32 [4096, 8], P(('groups', 'dev', 'sub')), parts along dimension 0, may hold values from 0 to 255, all different within a row; in each aligned block of 128 rows (0 to 127, 128 to 255, ...) at most 6 rows name the same one
- gate_values: float32 [4096, 8], P(('groups', 'dev', 'sub')), parts along dimension 0, may hold values from 0.05 to 1
- gate_proj: bfloat16 [16, 7168, 128], P(('dev', 'sub')), may hold values from -0.0625 to 0.0625
- up_proj: bfloat16 [16, 7168, 128], P(('dev', 'sub')), may hold values from -0.0625 to 0.0625
- down_proj: bfloat16 [16, 128, 7168], P(('dev', 'sub')), may hold values from -0.125 to 0.125
Outputs:
- moe_out: bfloat16 [4096, 7168], P(('groups', 'dev', 'sub')), parts along dimension 0
The draws below stay inside these ranges and needn't reach their ends.
There are 2 independent parts, one for each index of `groups`. The reference program is written for one: setup_inputs(seed, part) draws one part's arguments, and reference() takes and returns one part's arrays. A program takes and returns all parts, laid end to end along the dimension named above; an argument that names none is the same for every part. Nothing has to cross between parts.
Inputs may be any that keep to these rules, and one draw needn't show every extreme that they name: `expert_ids`: each row names 8 different experts; within the 128 rows of one device no expert is named by more than 6 rows.
All inputs are finite; a program needn't handle non-finite values.
Results may differ from the reference program's by a relative error of at most 0.0058.
Values may be sent and summed in bfloat16 or wider, within the bound.
A program may use at most 128 MiB of HBM per device.

```python
import math
import jax
import jax.numpy as jnp
import numpy as np
from jax import lax

D = 7168
H = 2048
E_ALL = 256
TOP = 8
SH = 16
TOK_DEV = 128
CAP = 6
EW = 1
HS = 128
TOKENS = 2048
N_DEV = 8
N_SUB = 2


def block_levels(stream_key, shape, pieces, low, largest):
    def one(axis_at, shards_of):
        heights = jax.random.uniform(jax.random.fold_in(jax.random.fold_in(stream_key, 6), axis_at), (shards_of,), jnp.float32, low / len(pieces), largest / len(pieces))
        return jnp.repeat(jnp.exp(heights), shape[axis_at] // shards_of).reshape((-1,) + (1,) * (len(shape) - axis_at - 1))

    gain = one(*pieces[0])
    for cut in pieces[1:]:
        gain = gain * one(*cut)
    return gain


def assign_block(own_key, own, number, rows, amount, top, most, lean):
    order = jax.random.permutation(own_key, amount)
    heavy_load, usual = load_shares(amount, rows * top, most, lean, True), load_shares(amount, rows * top, most, lean, False)
    places = jnp.arange(amount)

    def named(tallies, rotation):
        used = int((tallies > 0).sum())
        fixed = max(1, used // 4)
        moved = fixed + (places - fixed + rotation * (used - fixed)) % max(1, amount - fixed)
        return jnp.zeros((amount,), jnp.int32).at[order[jnp.where(places < fixed, places, moved)]].set(jnp.asarray(tallies, jnp.int32))

    tallies = jnp.where(number % 4 == 0, named(heavy_load, number // 4), named(usual, number - number // 4 - 1))
    mixed = jax.random.permutation(jax.random.fold_in(own, 3), amount)
    donor, taker = mixed[0:amount // 2 * 2:2], mixed[1:amount // 2 * 2:2]
    room = jnp.minimum(tallies[donor] - 1, most - tallies[taker]) // 2
    room = jnp.where((donor == order[0]) | (taker == order[0]) | (tallies[taker] == 0), 0, jnp.maximum(room, 0))
    moved = jax.random.randint(jax.random.fold_in(own, 4), (amount // 2,), 0, 1 << 20) % (room + 1)
    tallies = tallies.at[donor].add(-moved).at[taker].add(moved)
    labels = jnp.searchsorted(jnp.cumsum(tallies), jnp.arange(rows * top), side="right").astype(jnp.int32)
    listing = labels.reshape(top, rows).T
    listing = listing[jax.random.permutation(jax.random.fold_in(own, 1), rows)]
    rotation = jax.random.randint(jax.random.fold_in(own, 2), (rows, 1), 0, top)
    return jnp.take_along_axis(listing, (jnp.arange(top)[None, :] + rotation) % top, axis=1)


def load_shares(amount, total, bound, skew, full):
    weights = [(1 << 20) // math.isqrt(rank ** skew) + 1 for rank in range(1, amount + 1)]
    largest = bound if full else min(bound, max(-(-total // amount), total * weights[0] // sum(weights)))
    least = 1 if total - largest >= amount - 1 else 0
    given, rest = [largest] + [least] * (amount - 1), total - largest - least * (amount - 1)
    while rest > 0:
        candidates = [i for i in range(1, amount) if given[i] < largest] or [i for i in range(1, amount) if given[i] < bound]
        pool, remaining = sum([weights[i] for i in candidates]), rest
        for i in candidates:
            more = min(bound - given[i], max(1, remaining * weights[i] // pool), rest)
            given[i] = given[i] + more
            rest = rest - more
    return np.array(given)


def bell_draw(rng, dims, spread, reach, cuts=(), kind=jnp.bfloat16):
    factor_of = block_levels(rng, dims, cuts, -0.22, 0.18) if cuts else 1.0
    result = jax.random.normal(rng, dims, jnp.float32) * spread * factor_of
    return jnp.minimum(jnp.maximum(result, -reach), reach).astype(kind)


def setup_inputs(seed: int = 0, part: int = 0) -> dict:
    seeds = jax.random.split(jax.random.key(seed), 7)
    part_keys = jax.random.split(jax.random.fold_in(seeds[6], part), 7)
    tokens = bell_draw(part_keys[0], (TOKENS, D), 1.0, 6.0, ((0, 16),))
    expert_ids_keys = jax.random.split(jax.random.fold_in(part_keys[1], 1), TOKENS // TOK_DEV)
    expert_ids_turns = jax.random.permutation(jax.random.fold_in(part_keys[1], 3), TOKENS // TOK_DEV)
    expert_ids = jax.vmap(lambda own, number: assign_block(jax.random.fold_in(part_keys[1], 2), own, number, TOK_DEV, E_ALL, TOP, CAP, 2))(expert_ids_keys, expert_ids_turns).reshape((TOKENS, TOP))
    gate_values = jnp.clip(jnp.exp(math.log(1.0) - 2.9957323 * jax.random.uniform(part_keys[2], (TOKENS, TOP), jnp.float32) ** block_levels(part_keys[2], (TOKENS, TOP), ((0, 16),), -0.2, 0.2)), 0.05, 1.0)
    gate_proj = bell_draw(seeds[3], (N_DEV * N_SUB, D, HS), D ** -0.5, 0.0625, ((0, 16),))
    up_proj = bell_draw(seeds[4], (N_DEV * N_SUB, D, HS), D ** -0.5, 0.0625, ((0, 16),))
    down_proj = bell_draw(seeds[5], (N_DEV * N_SUB, HS, D), H ** -0.5, 0.125, ((0, 16),))
    return {"tokens": tokens, "expert_ids": expert_ids, "gate_values": gate_values, "gate_proj": gate_proj, "up_proj": up_proj, "down_proj": down_proj}


def plan(expert_ids, gate_values):
    experts = jnp.arange(EW, dtype=jnp.int32)
    matches = expert_ids[:, :, None] == experts[None, None, :]
    counts = jnp.sum(matches.astype(jnp.int32), axis=1)
    weight = jnp.sum(jnp.where(matches, gate_values[:, :, None], jnp.zeros_like(gate_values[:, :, None])), axis=1)
    ranking = jnp.cumsum(counts, axis=0) - 1
    slot_ids = jnp.arange(CAP, dtype=jnp.int32)
    chosen = (counts.T[:, None, :] == 1) & (ranking.T[:, None, :] == slot_ids[None, :, None])
    return chosen, weight


def expert_rows(row_block, gate_w, up_w, down_w):
    gate_act = jnp.dot(row_block, gate_w, preferred_element_type=jnp.float32)
    up_act = jnp.dot(row_block, up_w, preferred_element_type=jnp.float32)
    hidden = (jax.nn.silu(gate_act) * up_act).astype(jnp.bfloat16)
    return jnp.dot(hidden, down_w, preferred_element_type=jnp.float32).astype(jnp.bfloat16)


def reference(tokens, expert_ids, gate_values, gate_proj, up_proj, down_proj):
    blocks = N_DEV * N_SUB
    tok_blocks = tokens.reshape(blocks, TOK_DEV, D)
    chosen, weight = jax.vmap(plan)(expert_ids.reshape(blocks, TOK_DEV, TOP), gate_values.reshape(blocks, TOK_DEV, TOP))

    def dispatch_one(pair):
        chosen_one, tok_one = pair
        picked = chosen_one.astype(jnp.bfloat16).reshape(EW * CAP, TOK_DEV)
        return jnp.dot(picked, tok_one, preferred_element_type=jnp.float32).astype(jnp.bfloat16).reshape(EW, CAP, D)

    dispatched = lax.map(dispatch_one, (chosen, tok_blocks))
    stacked = jnp.moveaxis(dispatched, 1, 0)
    gate4 = gate_proj.reshape(EW, SH, D, HS)
    up4 = up_proj.reshape(EW, SH, D, HS)
    down4 = down_proj.reshape(EW, SH, HS, D)

    def per_expert(items):
        rows_e, gate_e, up_e, down_e = items
        row_block = rows_e.reshape(blocks * CAP, D)
        summed = jnp.zeros((blocks * CAP, D), jnp.float32)
        for shard_idx in range(SH):
            summed = summed + expert_rows(row_block, gate_e[shard_idx], up_e[shard_idx], down_e[shard_idx]).astype(jnp.float32)
        return summed.reshape(blocks, CAP, D)

    expert_out = jnp.moveaxis(lax.map(per_expert, (stacked, gate4, up4, down4)), 0, 1)
    combine = chosen.astype(jnp.float32) * jnp.transpose(weight, (0, 2, 1))[:, :, None, :]
    moe_out = jnp.einsum("pect,pecd->ptd", combine, expert_out, precision=lax.Precision.HIGHEST)
    return moe_out.astype(jnp.bfloat16).reshape(TOKENS, D)
```

```python
import functools

import jax
import jax.numpy as jnp
from jax import lax
from jax.experimental import pallas as pl
from jax.experimental.pallas import tpu as pltpu
from jax.sharding import PartitionSpec as P

SH = 16
CAP = 6
PARTS = 8
ROWS = PARTS * CAP
NZ = 4
F32 = jnp.float32
BF16 = jnp.bfloat16
MESH = pl.DeviceIdType.MESH


def iota(shape, dim):
    return lax.broadcasted_iota(jnp.int32, shape, dim)


def mm(a, b):
    return jnp.dot(a, b, preferred_element_type=F32)


def lane_plan(ids):
    tok = ids.shape[0]
    match = (ids == 0).astype(F32).astype(BF16)
    ones = jnp.ones((ROWS, ids.shape[1]), BF16)
    count = lax.dot_general(ones, match, (((1,), (1,)), ((), ())), preferred_element_type=F32)
    upper = (iota((tok, tok), 0) <= iota((tok, tok), 1)).astype(F32).astype(BF16)
    rank = mm(count.astype(BF16), upper)
    return count > 0.5, (rank + 0.5).astype(jnp.int32) - 1


def move_matrix(transposed):
    big, small = PARTS * 32, NZ * ROWS
    shape = (small, big) if transposed else (big, small)
    a = iota(shape, 1 if transposed else 0)
    b = iota(shape, 0 if transposed else 1)
    p, j, r = a >> 5, (a >> 3) & 3, a & 7
    return ((b == j * ROWS + p * CAP + r) & (r < CAP)).astype(F32).astype(BF16)


def moe_kernel(ids_ref, tok_hbm, gate_hbm, up_hbm, down_hbm, out_ref,
               tok, gu, dn, wire, xbuf, ybuf, part, sib_in, y_in, y_out, zu_in, zd_in, zu_out, zd_out,
               loc, ag_recv, ag_up, ag_down, ag_y, ag_sib,
               s_send, s_recv, y_send, y_recv, zu_send, zu_recv, zd_send, zd_recv):
    width = wire.shape[2]
    g, dev, c = lax.axis_index("groups"), lax.axis_index("dev"), lax.axis_index("sub")
    z, y = dev // 2, dev % 2
    up_dev, down_dev = (g, dev + 2, c), (g, dev - 2, c)
    y_dev, sib_dev = (g, z * 2 + 1 - y, c), (g, dev, 1 - c)

    barrier = pltpu.get_barrier_semaphore()

    def greet(device):
        pl.semaphore_signal(barrier, inc=1, device_id=device, device_id_type=MESH)

    load_tok = pltpu.make_async_copy(tok_hbm, tok, loc.at[0])
    load_gate = pltpu.make_async_copy(gate_hbm.at[0], gu.at[:, 0:128], loc.at[1])
    load_up = pltpu.make_async_copy(up_hbm.at[0], gu.at[:, 128:256], loc.at[2])
    load_down = pltpu.make_async_copy(down_hbm.at[0], dn, loc.at[3])
    load_tok.start()
    greet(sib_dev)
    greet(y_dev)
    pl.when(z < NZ - 1)(lambda: greet(up_dev))
    pl.when(z > 0)(lambda: greet(down_dev))
    load_gate.start()
    load_up.start()
    load_down.start()

    def remote(src, dst, ss, rs, device):
        return pltpu.make_async_remote_copy(
            src_ref=src, dst_ref=dst, send_sem=ss, recv_sem=rs, device_id=device, device_id_type=MESH)

    def slot(zz, yy, cc):
        return zz * 4 + yy * 2 + cc

    def gather(zz, yy, ss, device):
        s = slot(zz, yy, c)
        return remote(wire.at[s], wire.at[s], ss, ag_recv.at[s], device)

    def to_up(zz):
        return gather(zz, y, ag_up.at[zz], up_dev)

    def to_down(zz):
        return gather(zz, y, ag_down.at[zz], down_dev)

    def to_y(zz):
        return gather(zz, y, ag_y.at[zz], y_dev)

    def to_sib(zz, yy):
        return gather(zz, yy, ag_sib.at[zz * 2 + yy], sib_dev)

    def arrived(zz, yy, cc):
        s = slot(zz, yy, cc)
        remote(wire.at[s], wire.at[s], ag_y.at[0], ag_recv.at[s], y_dev).wait_recv()

    count, place = lane_plan(ids_ref[...])
    row = iota(place.shape, 0)
    load_tok.wait()
    acc = jnp.zeros((ROWS, width), F32)
    for p in range(PARTS):
        r = row - p * CAP
        sel = (count & (place == r) & (r >= 0) & (r < CAP)).astype(F32).astype(BF16)
        acc += mm(sel, tok[:, p * width:(p + 1) * width])
    wire[slot(z, y, c)] = acc.astype(BF16)

    pl.semaphore_wait(barrier, 2 + (z + NZ - 2) // (NZ - 1) + (2 * NZ - 3 - z) // (NZ - 1))

    pl.when(z < NZ - 1)(lambda: to_up(z).start())
    pl.when(z > 0)(lambda: to_down(z).start())
    to_y(z).start()
    to_sib(z, y).start()

    def relay_up(zz):
        arrived(zz, y, c)
        pl.when(z < NZ - 1)(lambda: to_up(zz).start())
        to_y(zz).start()
        to_sib(zz, y).start()

    def relay_down(zz):
        arrived(zz, y, c)
        pl.when(z > 0)(lambda: to_down(zz).start())
        to_y(zz).start()
        to_sib(zz, y).start()

    def relay_sib(zz):
        arrived(zz, 1 - y, c)
        to_sib(zz, 1 - y).start()

    for d in range(1, NZ + 1):
        if d < NZ:
            pl.when(z - d >= 0)(functools.partial(relay_up, z - d))
            pl.when(z + d < NZ)(functools.partial(relay_down, z + d))
        if d == 1:
            relay_sib(z)
        else:
            pl.when(z - (d - 1) >= 0)(functools.partial(relay_sib, z - (d - 1)))
            pl.when(z + (d - 1) < NZ)(functools.partial(relay_sib, z + (d - 1)))

    half = z // 2
    far = NZ - 1 - (NZ - 1) * half
    mid = 2 - half
    order = (far, mid, 6 - far - mid - z, z)

    move = move_matrix(False)
    for zz in order[::-1]:
        arrived(zz, 0, 1 - c)
        arrived(zz, 1, 1 - c)
        rows = mm(move, wire[pl.ds(zz * 4, 4)].reshape(4 * ROWS, width)).astype(BF16)
        for p in range(PARTS):
            xbuf[pl.ds(pl.multiple_of(zz * 32, 32), 32), p * width:(p + 1) * width] = rows[p * 32:(p + 1) * 32]

    load_gate.wait()
    load_up.wait()
    act = jnp.zeros((NZ * 32, 256), F32)
    for p in range(PARTS):
        act += mm(xbuf[:, p * width:(p + 1) * width], gu[p * width:(p + 1) * width, :])
    gate, upv = act[:, :128], act[:, 128:]
    hidden = (gate / (1.0 + jnp.exp(-gate)) * upv).astype(BF16)

    load_down.wait()
    for p in range(PARTS):
        val = mm(hidden, dn[:, p * width:(p + 1) * width]).astype(BF16)
        for zz in range(NZ):
            ybuf[zz, p * 32:(p + 1) * 32] = val[zz * 32:(zz + 1) * 32]

    def s_copy(zz, yy):
        k = zz * 2 + yy
        return remote(part.at[slot(zz, yy, 1 - c)], sib_in.at[k], s_send.at[k], s_recv.at[k], sib_dev)

    def y_copy(zz):
        return remote(y_out.at[zz], y_in.at[zz], y_send.at[zz], y_recv.at[zz], y_dev)

    def zu_copy(zz):
        return remote(zu_out.at[zz], zu_in.at[zz], zu_send.at[zz], zu_recv.at[zz], up_dev)

    def zd_copy(zz):
        return remote(zd_out.at[zz], zd_in.at[zz], zd_send.at[zz], zd_recv.at[zz], down_dev)

    back = move_matrix(True)
    for zz in order:
        vals = mm(back, ybuf[zz]).astype(BF16)
        part[pl.ds(zz * 4, 4)] = vals.reshape(4, ROWS, width)
        s_copy(zz, 1 - y).start()
        s_copy(zz, y).start()

    for zz in order:
        s_copy(zz, 1 - y).wait_recv()
        y_out[zz] = (part[slot(zz, 1 - y, c)].astype(F32) + sib_in[zz * 2 + 1 - y].astype(F32)).astype(BF16)
        y_copy(zz).start()

    def mine(zz):
        s_copy(zz, y).wait_recv()
        y_copy(zz).wait_recv()
        return part[slot(zz, y, c)].astype(F32) + sib_in[zz * 2 + y].astype(F32) + y_in[zz].astype(F32)

    def send_up(zz):
        zu_out[zz] = mine(zz).astype(BF16)

        @pl.when(z > 0)
        def _():
            zu_copy(zz).wait_recv()
            zu_out[zz] = (zu_out[zz].astype(F32) + zu_in[zz].astype(F32)).astype(BF16)

        zu_copy(zz).start()

    def send_down(zz):
        zd_out[zz] = mine(zz).astype(BF16)

        @pl.when(z < NZ - 1)
        def _():
            zd_copy(zz).wait_recv()
            zd_out[zz] = (zd_out[zz].astype(F32) + zd_in[zz].astype(F32)).astype(BF16)

        zd_copy(zz).start()

    for d in range(NZ - 1, 0, -1):
        pl.when(z + d < NZ)(functools.partial(send_up, z + d))
        pl.when(z - d >= 0)(functools.partial(send_down, z - d))
    out_ref[...] = mine(z)

    @pl.when(z > 0)
    def _():
        zu_copy(z).wait_recv()
        out_ref[...] += zu_in[z].astype(F32)

    @pl.when(z < NZ - 1)
    def _():
        zd_copy(z).wait_recv()
        out_ref[...] += zd_in[z].astype(F32)

    for zz in range(NZ):
        pl.when((z < NZ - 1) & (zz <= z))(functools.partial(lambda k: to_up(k).wait_send(), zz))
        pl.when((z > 0) & (zz >= z))(functools.partial(lambda k: to_down(k).wait_send(), zz))
        to_y(zz).wait_send()
        y_copy(zz).wait_send()
        for yy in range(2):
            to_sib(zz, yy).wait_send()
            s_copy(zz, yy).wait_send()
        pl.when(zz > z)(functools.partial(lambda k: zu_copy(k).wait_send(), zz))
        pl.when(zz < z)(functools.partial(lambda k: zd_copy(k).wait_send(), zz))


def spread_kernel(ids_ref, gates_ref, merged_ref, out_hbm, stage, sems):
    ids = ids_ref[...]
    tok, width = ids.shape[0], merged_ref.shape[1]
    hit = ids == 0
    match = hit.astype(F32)
    weight = jnp.sum(jnp.where(hit, gates_ref[...], 0.0), axis=1, keepdims=True)
    count = jnp.sum(match, axis=1, keepdims=True) > 0.5
    lower = (iota((tok, tok), 0) >= iota((tok, tok), 1)).astype(F32).astype(BF16)
    rank = jnp.sum(mm(lower, match.astype(BF16)), axis=1, keepdims=True)
    place = (rank + 0.5).astype(jnp.int32) - 1
    merged = merged_ref[...]
    high = merged.astype(BF16)
    rest = merged - high.astype(F32)
    middle = rest.astype(BF16)
    low = (rest - middle.astype(F32)).astype(BF16)
    col = iota((tok, ROWS), 1)
    copies = []
    for p in range(PARTS):
        r = col - p * CAP
        sel = (count & (place == r) & (r >= 0) & (r < CAP)).astype(F32).astype(BF16)
        val = (mm(sel, high) + mm(sel, middle)) + mm(sel, low)
        stage[:, p * width:(p + 1) * width] = (val * weight).astype(BF16)
        cols = pl.ds(p * width, width)
        copy = pltpu.make_async_copy(stage.at[:, cols], out_hbm.at[:, cols], sems.at[p])
        copy.start()
        copies.append(copy)
    for copy in copies:
        copy.wait()


def fast(tokens, expert_ids, gate_values, gate_proj, up_proj, down_proj):
    tok, model = tokens.shape
    width = model // PARTS
    vmem = pl.BlockSpec(memory_space=pltpu.VMEM)
    hbm = pl.BlockSpec(memory_space=pl.ANY)
    dma = pltpu.SemaphoreType.DMA

    def blocks(n):
        return pltpu.VMEM((n, ROWS, width), BF16)

    merged = pl.pallas_call(
        moe_kernel,
        out_shape=jax.ShapeDtypeStruct((ROWS, width), F32),
        in_specs=[vmem, hbm, hbm, hbm, hbm],
        out_specs=vmem,
        scratch_shapes=[
            pltpu.VMEM((tok, model), BF16),
            pltpu.VMEM((model, 256), BF16),
            pltpu.VMEM((128, model), BF16),
            blocks(SH),
            pltpu.VMEM((NZ * 32, model), BF16),
            pltpu.VMEM((NZ, PARTS * 32, width), BF16),
            blocks(SH), blocks(8), blocks(NZ), blocks(NZ), blocks(NZ), blocks(NZ), blocks(NZ), blocks(NZ),
            dma((4,)), dma((SH,)), dma((NZ,)), dma((NZ,)), dma((NZ,)), dma((8,)),
            dma((8,)), dma((8,)), dma((NZ,)), dma((NZ,)), dma((NZ,)), dma((NZ,)), dma((NZ,)), dma((NZ,)),
        ],
        compiler_params=pltpu.CompilerParams(
            collective_id=0, has_side_effects=True, vmem_limit_bytes=48 * 1024 * 1024),
        name="expert",
    )(expert_ids, tokens, gate_proj, up_proj, down_proj)
    return pl.pallas_call(
        spread_kernel,
        out_shape=jax.ShapeDtypeStruct((tok, model), BF16),
        in_specs=[vmem, vmem, vmem],
        out_specs=hbm,
        scratch_shapes=[pltpu.VMEM((tok, model), BF16), dma((PARTS,))],
        compiler_params=pltpu.CompilerParams(vmem_limit_bytes=32 * 1024 * 1024),
        name="spread",
    )(expert_ids, gate_values, merged)


def plan(expert_ids, gate_values, window):
    experts = jnp.arange(window, dtype=jnp.int32)
    matches = expert_ids[:, :, None] == experts[None, None, :]
    counts = jnp.sum(matches.astype(jnp.int32), axis=1)
    weight = jnp.sum(
        jnp.where(matches, gate_values[:, :, None], jnp.zeros_like(gate_values[:, :, None])), axis=1
    )
    ranking = jnp.cumsum(counts, axis=0) - 1
    slot_ids = jnp.arange(CAP, dtype=jnp.int32)
    chosen = (counts.T[:, None, :] == 1) & (ranking.T[:, None, :] == slot_ids[None, :, None])
    return (chosen, weight)


def general(tokens, expert_ids, gate_values, gate_proj, up_proj, down_proj):
    devices = lax.axis_size("dev") * lax.axis_size("sub")
    window = devices // SH
    model_width = tokens.shape[1]
    chosen, weight = plan(expert_ids, gate_values, window)
    picked = chosen.astype(jnp.bfloat16).reshape(window * CAP, tokens.shape[0])
    outbound = jnp.dot(picked, tokens, preferred_element_type=jnp.float32).astype(jnp.bfloat16)
    outbound = outbound.reshape(window, 1, CAP, model_width)
    sendbuf = jnp.broadcast_to(outbound, (window, SH, CAP, model_width)).reshape(
        devices, CAP, model_width
    )
    arrived = lax.all_to_all(sendbuf, ("dev", "sub"), split_axis=0, concat_axis=0, tiled=True)
    row_block = arrived.reshape(devices * CAP, model_width)
    gate_act = jnp.dot(row_block, gate_proj[0], preferred_element_type=jnp.float32)
    up_act = jnp.dot(row_block, up_proj[0], preferred_element_type=jnp.float32)
    hidden = (jax.nn.silu(gate_act) * up_act).astype(jnp.bfloat16)
    partial_value = jnp.dot(hidden, down_proj[0], preferred_element_type=jnp.float32).astype(
        jnp.bfloat16
    )
    returned = lax.all_to_all(
        partial_value.reshape(devices, CAP, model_width),
        ("dev", "sub"),
        split_axis=0,
        concat_axis=0,
        tiled=True,
    )
    merged = jnp.sum(returned.reshape(window, SH, CAP, model_width).astype(jnp.float32), axis=1)
    combine = (chosen.astype(jnp.float32) * weight.T[:, None, :]).reshape(
        window * CAP, tokens.shape[0]
    )
    moe_out = jnp.dot(
        combine.T,
        merged.reshape(window * CAP, model_width),
        precision=lax.Precision.HIGHEST,
        preferred_element_type=jnp.float32,
    )
    return moe_out.astype(jnp.bfloat16)


def solution(mesh):
    placed = (
        P(("groups", "dev", "sub"), None),
        P(("groups", "dev", "sub"), None),
        P(("groups", "dev", "sub"), None),
        P(("dev", "sub"), None, None),
        P(("dev", "sub"), None, None),
        P(("dev", "sub"), None, None),
    )
    one_expert = mesh.shape["dev"] == 2 * NZ and mesh.shape["sub"] == 2
    return jax.shard_map(
        fast if one_expert else general,
        mesh=mesh,
        in_specs=placed,
        out_specs=P(("groups", "dev", "sub"), None),
        check_vma=False,
    )
```

```python
import functools

import jax
import jax.numpy as jnp
from jax import lax
from jax.experimental import pallas as pl
from jax.experimental.pallas import tpu as pltpu
from jax.sharding import PartitionSpec as P

SH = 16
CAP = 6
PARTS = 8
ROWS = PARTS * CAP
NZ = 4
NC = 3
PIECE = ROWS // NC
F32 = jnp.float32
BF16 = jnp.bfloat16
MESH = pl.DeviceIdType.MESH


def iota(shape, dim):
    return lax.broadcasted_iota(jnp.int32, shape, dim)


def mm(a, b):
    return jnp.dot(a, b, preferred_element_type=F32)


def lane_plan(ids):
    tok = ids.shape[1]
    match = (ids == 0).astype(F32).astype(BF16)
    count = mm(jnp.ones((ROWS, ids.shape[0]), BF16), match)
    upper = (iota((tok, tok), 0) <= iota((tok, tok), 1)).astype(F32).astype(BF16)
    rank = mm(count.astype(BF16), upper)
    return count > 0.5, (rank + 0.5).astype(jnp.int32) - 1


def move_matrix(transposed):
    big, small = PARTS * 32, NZ * ROWS
    shape = (small, big) if transposed else (big, small)
    a = iota(shape, 1 if transposed else 0)
    b = iota(shape, 0 if transposed else 1)
    p, j, r = a >> 5, (a >> 3) & 3, a & 7
    return ((b == j * ROWS + p * CAP + r) & (r < CAP)).astype(F32).astype(BF16)


def moe_kernel(ids_hbm, gates_hbm, tok_hbm, gate_hbm, up_hbm, down_hbm, out_ref, place_ref, weight_ref,
               ids_v, gates_v, tok, gu, dn, wire, xbuf, ybuf, part, sib_in, y_in, y_out, zu_in, zd_in, zu_out, zd_out,
               loc, ag_recv, ag_up, ag_down, ag_y, ag_sib,
               s_send, s_recv, y_send, y_recv, zu_send, zu_recv, zd_send, zd_recv):
    width = wire.shape[2]
    g, dev, c = lax.axis_index("groups"), lax.axis_index("dev"), lax.axis_index("sub")
    z, y = dev // 2, dev % 2
    up_dev, down_dev = (g, dev + 2, c), (g, dev - 2, c)
    y_dev, sib_dev = (g, z * 2 + 1 - y, c), (g, dev, 1 - c)

    barrier = pltpu.get_barrier_semaphore()

    def greet(device):
        pl.semaphore_signal(barrier, inc=1, device_id=device, device_id_type=MESH)

    load_tok = pltpu.make_async_copy(tok_hbm, tok, loc.at[0])
    load_gate = pltpu.make_async_copy(gate_hbm.at[0], gu.at[:, 0:128], loc.at[1])
    load_up = pltpu.make_async_copy(up_hbm.at[0], gu.at[:, 128:256], loc.at[2])
    load_down = pltpu.make_async_copy(down_hbm.at[0], dn, loc.at[3])
    load_ids = pltpu.make_async_copy(ids_hbm, ids_v, loc.at[4])
    load_gates = pltpu.make_async_copy(gates_hbm, gates_v, loc.at[5])
    load_ids.start()
    load_tok.start()
    load_gates.start()
    greet(sib_dev)
    greet(y_dev)
    pl.when(z < NZ - 1)(lambda: greet(up_dev))
    pl.when(z > 0)(lambda: greet(down_dev))
    load_gate.start()
    load_up.start()
    load_down.start()

    def remote(src, dst, ss, rs, device):
        return pltpu.make_async_remote_copy(
            src_ref=src, dst_ref=dst, send_sem=ss, recv_sem=rs, device_id=device, device_id_type=MESH)

    def slot(zz, yy, cc):
        return zz * 4 + yy * 2 + cc

    def gather(zz, yy, k, ss, device):
        piece = wire.at[slot(zz, yy, c), pl.ds(k * PIECE, PIECE)]
        return remote(piece, piece, ss, ag_recv.at[slot(zz, yy, c) * NC + k], device)

    def to_up(zz, k):
        return gather(zz, y, k, ag_up.at[zz * NC + k], up_dev)

    def to_down(zz, k):
        return gather(zz, y, k, ag_down.at[zz * NC + k], down_dev)

    def to_y(zz, k):
        return gather(zz, y, k, ag_y.at[zz * NC + k], y_dev)

    def to_sib(zz, yy, k):
        return gather(zz, yy, k, ag_sib.at[(zz * 2 + yy) * NC + k], sib_dev)

    def arrived(zz, yy, cc, k):
        piece = wire.at[slot(zz, yy, cc), pl.ds(k * PIECE, PIECE)]
        remote(piece, piece, ag_y.at[0], ag_recv.at[slot(zz, yy, cc) * NC + k], y_dev).wait_recv()

    load_ids.wait()
    count, place = lane_plan(ids_v[...])
    row = iota(place.shape, 0)
    load_tok.wait()
    acc = jnp.zeros((ROWS, width), F32)
    for p in range(PARTS):
        r = row - p * CAP
        sel = (count & (place == r) & (r >= 0) & (r < CAP)).astype(F32).astype(BF16)
        acc += mm(sel, tok[:, p * width:(p + 1) * width])
    wire[slot(z, y, c)] = acc.astype(BF16)

    pl.semaphore_wait(barrier, 2 + (z + NZ - 2) // (NZ - 1) + (2 * NZ - 3 - z) // (NZ - 1))

    def first_up(k):
        pl.when(z < NZ - 1)(lambda: to_up(z, k).start())

    def first_down(k):
        pl.when(z > 0)(lambda: to_down(z, k).start())

    for k in range(NC):
        first_up(k)
        first_down(k)
        to_y(z, k).start()
    for k in range(NC):
        to_sib(z, y, k).start()

    def relay_up(zz, k):
        arrived(zz, y, c, k)
        pl.when(z < NZ - 1)(lambda: to_up(zz, k).start())
        to_y(zz, k).start()
        to_sib(zz, y, k).start()

    def relay_down(zz, k):
        arrived(zz, y, c, k)
        pl.when(z > 0)(lambda: to_down(zz, k).start())
        to_y(zz, k).start()
        to_sib(zz, y, k).start()

    def relay_sib(zz, k):
        arrived(zz, 1 - y, c, k)
        to_sib(zz, 1 - y, k).start()

    load_gates.wait()
    ids, gate_cols = ids_v[...].T, gates_v[...].T
    tokens = ids.shape[0]
    hit = ids == 0
    match = hit.astype(F32)
    weight = jnp.sum(jnp.where(hit, gate_cols, 0.0), axis=1, keepdims=True)
    named = jnp.sum(match, axis=1, keepdims=True) > 0.5
    lower = (iota((tokens, tokens), 0) >= iota((tokens, tokens), 1)).astype(F32).astype(BF16)
    rank = jnp.sum(mm(lower, match.astype(BF16)), axis=1, keepdims=True)
    taken = (rank + 0.5).astype(jnp.int32) - 1
    taken = jnp.where(named & (taken < CAP), taken, -ROWS)
    place_ref[...] = jnp.broadcast_to(taken, place_ref.shape)
    weight_ref[...] = jnp.broadcast_to(weight, weight_ref.shape)

    for d in range(1, NZ + 1):
        for k in range(NC):
            if d < NZ:
                pl.when(z - d >= 0)(functools.partial(relay_up, z - d, k))
                pl.when(z + d < NZ)(functools.partial(relay_down, z + d, k))
            if d == 1:
                relay_sib(z, k)
            else:
                pl.when(z - (d - 1) >= 0)(functools.partial(relay_sib, z - (d - 1), k))
                pl.when(z + (d - 1) < NZ)(functools.partial(relay_sib, z + (d - 1), k))

    half = z // 2
    far = NZ - 1 - (NZ - 1) * half
    mid = 2 - half
    order = (far, mid, 6 - far - mid - z, z)

    move = move_matrix(False)
    for zz in order[::-1]:
        for k in range(NC):
            arrived(zz, 0, 1 - c, k)
            arrived(zz, 1, 1 - c, k)
        rows = mm(move, wire[pl.ds(zz * 4, 4)].reshape(4 * ROWS, width)).astype(BF16)
        for p in range(PARTS):
            xbuf[pl.ds(pl.multiple_of(zz * 32, 32), 32), p * width:(p + 1) * width] = rows[p * 32:(p + 1) * 32]

    load_gate.wait()
    load_up.wait()
    act = jnp.zeros((NZ * 32, 256), F32)
    for p in range(PARTS):
        act += mm(xbuf[:, p * width:(p + 1) * width], gu[p * width:(p + 1) * width, :])
    gate, upv = act[:, :128], act[:, 128:]
    hidden = (gate / (1.0 + jnp.exp(-gate)) * upv).astype(BF16)

    load_down.wait()
    for p in range(PARTS):
        val = mm(hidden, dn[:, p * width:(p + 1) * width]).astype(BF16)
        for zz in range(NZ):
            ybuf[zz, p * 32:(p + 1) * 32] = val[zz * 32:(zz + 1) * 32]

    def rows_of(k):
        return pl.ds(k * PIECE, PIECE)

    def s_copy(zz, yy, k):
        n = (zz * 2 + yy) * NC + k
        return remote(part.at[slot(zz, yy, 1 - c), rows_of(k)], sib_in.at[zz * 2 + yy, rows_of(k)],
                      s_send.at[n], s_recv.at[n], sib_dev)

    def line(src, dst, ss, rs, device):
        def copy(zz, k):
            n = zz * NC + k
            return remote(src.at[zz, rows_of(k)], dst.at[zz, rows_of(k)], ss.at[n], rs.at[n], device)
        return copy

    y_copy = line(y_out, y_in, y_send, y_recv, y_dev)
    zu_copy = line(zu_out, zu_in, zu_send, zu_recv, up_dev)
    zd_copy = line(zd_out, zd_in, zd_send, zd_recv, down_dev)

    back = move_matrix(True)
    for zz in order:
        vals = mm(back, ybuf[zz]).astype(BF16)
        part[pl.ds(zz * 4, 4)] = vals.reshape(4, ROWS, width)
        for yy in (1 - y, y):
            for k in range(NC):
                s_copy(zz, yy, k).start()

    for zz in order:
        for k in range(NC):
            s_copy(zz, 1 - y, k).wait_recv()
            at = rows_of(k)
            y_out[zz, at] = (part[slot(zz, 1 - y, c), at].astype(F32) + sib_in[zz * 2 + 1 - y, at].astype(F32)).astype(BF16)
            y_copy(zz, k).start()

    def mine(zz, k):
        s_copy(zz, y, k).wait_recv()
        y_copy(zz, k).wait_recv()
        at = rows_of(k)
        return part[slot(zz, y, c), at].astype(F32) + sib_in[zz * 2 + y, at].astype(F32) + y_in[zz, at].astype(F32)

    def send_line(copy, out, inn, inner, zz, k):
        at = rows_of(k)
        out[zz, at] = mine(zz, k).astype(BF16)

        @pl.when(inner)
        def _():
            copy(zz, k).wait_recv()
            out[zz, at] = (mine_again(zz, k) + inn[zz, at].astype(F32)).astype(BF16)

        copy(zz, k).start()

    def mine_again(zz, k):
        at = rows_of(k)
        return part[slot(zz, y, c), at].astype(F32) + sib_in[zz * 2 + y, at].astype(F32) + y_in[zz, at].astype(F32)

    for d in range(NZ - 1, 0, -1):
        for k in range(NC):
            pl.when(z + d < NZ)(functools.partial(send_line, zu_copy, zu_out, zu_in, z > 0, z + d, k))
            pl.when(z - d >= 0)(functools.partial(send_line, zd_copy, zd_out, zd_in, z < NZ - 1, z - d, k))
    for k in range(NC):
        out_ref[rows_of(k)] = mine(z, k)

    @pl.when(z > 0)
    def _():
        for k in range(NC):
            zu_copy(z, k).wait_recv()
            out_ref[rows_of(k)] += zu_in[z, rows_of(k)].astype(F32)

    @pl.when(z < NZ - 1)
    def _():
        for k in range(NC):
            zd_copy(z, k).wait_recv()
            out_ref[rows_of(k)] += zd_in[z, rows_of(k)].astype(F32)

    def left(copy, zz, k):
        copy(zz, k).wait_send()

    for zz in range(NZ):
        for k in range(NC):
            pl.when((z < NZ - 1) & (zz <= z))(functools.partial(left, to_up, zz, k))
            pl.when((z > 0) & (zz >= z))(functools.partial(left, to_down, zz, k))
            to_y(zz, k).wait_send()
            y_copy(zz, k).wait_send()
            for yy in range(2):
                to_sib(zz, yy, k).wait_send()
                s_copy(zz, yy, k).wait_send()
            pl.when(zz > z)(functools.partial(left, zu_copy, zz, k))
            pl.when(zz < z)(functools.partial(left, zd_copy, zz, k))


def spread_kernel(place_ref, weight_ref, merged_ref, out_hbm, stage, sems):
    tok, width = place_ref.shape[0], merged_ref.shape[1]
    place, weight = place_ref[:, :ROWS], weight_ref[:, :1]
    merged = merged_ref[...]
    high = merged.astype(BF16)
    rest = merged - high.astype(F32)
    middle = rest.astype(BF16)
    low = (rest - middle.astype(F32)).astype(BF16)
    col = iota((tok, ROWS), 1)
    copies = []
    for p in range(PARTS):
        sel = (place == col - p * CAP).astype(F32).astype(BF16)
        val = (mm(sel, high) + mm(sel, middle)) + mm(sel, low)
        stage[:, p * width:(p + 1) * width] = (val * weight).astype(BF16)
        cols = pl.ds(p * width, width)
        copy = pltpu.make_async_copy(stage.at[:, cols], out_hbm.at[:, cols], sems.at[p])
        copy.start()
        copies.append(copy)
    for copy in copies:
        copy.wait()


def fast(tokens, expert_ids, gate_values, gate_proj, up_proj, down_proj):
    tok, model = tokens.shape
    width = model // PARTS
    ids, gates = expert_ids.T, gate_values.T
    vmem = pl.BlockSpec(memory_space=pltpu.VMEM)
    hbm = pl.BlockSpec(memory_space=pltpu.HBM)
    dma = pltpu.SemaphoreType.DMA

    def blocks(n):
        return pltpu.VMEM((n, ROWS, width), BF16)

    merged, place, weight = pl.pallas_call(
        moe_kernel,
        out_shape=(jax.ShapeDtypeStruct((ROWS, width), F32), jax.ShapeDtypeStruct((tok, 128), jnp.int32),
                   jax.ShapeDtypeStruct((tok, 128), F32)),
        in_specs=[hbm] * 6,
        out_specs=(vmem, vmem, vmem),
        scratch_shapes=[
            pltpu.VMEM(ids.shape, jnp.int32),
            pltpu.VMEM(gates.shape, F32),
            pltpu.VMEM((tok, model), BF16),
            pltpu.VMEM((model, 256), BF16),
            pltpu.VMEM((128, model), BF16),
            blocks(SH),
            pltpu.VMEM((NZ * 32, model), BF16),
            pltpu.VMEM((NZ, PARTS * 32, width), BF16),
            blocks(SH), blocks(8), blocks(NZ), blocks(NZ), blocks(NZ), blocks(NZ), blocks(NZ), blocks(NZ),
            dma((6,)), dma((SH * NC,)), dma((NZ * NC,)), dma((NZ * NC,)), dma((NZ * NC,)), dma((8 * NC,)),
            dma((8 * NC,)), dma((8 * NC,)), dma((NZ * NC,)), dma((NZ * NC,)),
            dma((NZ * NC,)), dma((NZ * NC,)), dma((NZ * NC,)), dma((NZ * NC,)),
        ],
        compiler_params=pltpu.CompilerParams(
            collective_id=0, has_side_effects=True, vmem_limit_bytes=60 * 1024 * 1024),
        name="expert",
    )(ids, gates, tokens, gate_proj, up_proj, down_proj)
    return pl.pallas_call(
        spread_kernel,
        out_shape=jax.ShapeDtypeStruct((tok, model), BF16),
        in_specs=[vmem, vmem, vmem],
        out_specs=hbm,
        scratch_shapes=[pltpu.VMEM((tok, model), BF16), dma((PARTS,))],
        compiler_params=pltpu.CompilerParams(vmem_limit_bytes=32 * 1024 * 1024),
        name="spread",
    )(place, weight, merged)


def plan(expert_ids, gate_values, window):
    experts = jnp.arange(window, dtype=jnp.int32)
    matches = expert_ids[:, :, None] == experts[None, None, :]
    counts = jnp.sum(matches.astype(jnp.int32), axis=1)
    weight = jnp.sum(
        jnp.where(matches, gate_values[:, :, None], jnp.zeros_like(gate_values[:, :, None])), axis=1
    )
    ranking = jnp.cumsum(counts, axis=0) - 1
    slot_ids = jnp.arange(CAP, dtype=jnp.int32)
    chosen = (counts.T[:, None, :] == 1) & (ranking.T[:, None, :] == slot_ids[None, :, None])
    return (chosen, weight)


def general(tokens, expert_ids, gate_values, gate_proj, up_proj, down_proj):
    devices = lax.axis_size("dev") * lax.axis_size("sub")
    window = devices // SH
    model_width = tokens.shape[1]
    chosen, weight = plan(expert_ids, gate_values, window)
    picked = chosen.astype(jnp.bfloat16).reshape(window * CAP, tokens.shape[0])
    outbound = jnp.dot(picked, tokens, preferred_element_type=jnp.float32).astype(jnp.bfloat16)
    outbound = outbound.reshape(window, 1, CAP, model_width)
    sendbuf = jnp.broadcast_to(outbound, (window, SH, CAP, model_width)).reshape(
        devices, CAP, model_width
    )
    arrived = lax.all_to_all(sendbuf, ("dev", "sub"), split_axis=0, concat_axis=0, tiled=True)
    row_block = arrived.reshape(devices * CAP, model_width)
    gate_act = jnp.dot(row_block, gate_proj[0], preferred_element_type=jnp.float32)
    up_act = jnp.dot(row_block, up_proj[0], preferred_element_type=jnp.float32)
    hidden = (jax.nn.silu(gate_act) * up_act).astype(jnp.bfloat16)
    partial_value = jnp.dot(hidden, down_proj[0], preferred_element_type=jnp.float32).astype(
        jnp.bfloat16
    )
    returned = lax.all_to_all(
        partial_value.reshape(devices, CAP, model_width),
        ("dev", "sub"),
        split_axis=0,
        concat_axis=0,
        tiled=True,
    )
    merged = jnp.sum(returned.reshape(window, SH, CAP, model_width).astype(jnp.float32), axis=1)
    combine = (chosen.astype(jnp.float32) * weight.T[:, None, :]).reshape(
        window * CAP, tokens.shape[0]
    )
    moe_out = jnp.dot(
        combine.T,
        merged.reshape(window * CAP, model_width),
        precision=lax.Precision.HIGHEST,
        preferred_element_type=jnp.float32,
    )
    return moe_out.astype(jnp.bfloat16)


def solution(mesh):
    placed = (
        P(("groups", "dev", "sub"), None),
        P(("groups", "dev", "sub"), None),
        P(("groups", "dev", "sub"), None),
        P(("dev", "sub"), None, None),
        P(("dev", "sub"), None, None),
        P(("dev", "sub"), None, None),
    )
    one_expert = mesh.shape["dev"] == 2 * NZ and mesh.shape["sub"] == 2
    return jax.shard_map(
        fast if one_expert else general,
        mesh=mesh,
        in_specs=placed,
        out_specs=P(("groups", "dev", "sub"), None),
        check_vma=False,
    )
```

```python
import functools

import jax
import jax.numpy as jnp
from jax import lax
from jax.experimental import pallas as pl
from jax.experimental.pallas import tpu as pltpu
from jax.sharding import PartitionSpec as P

SH = 16
CAP = 6
PARTS = 8
ROWS = PARTS * CAP
NZ = 4
NC = 3
PIECE = ROWS // NC
F32 = jnp.float32
BF16 = jnp.bfloat16
MESH = pl.DeviceIdType.MESH


def iota(shape, dim):
    return lax.broadcasted_iota(jnp.int32, shape, dim)


def mm(a, b):
    return jnp.dot(a, b, preferred_element_type=F32)


def lane_plan(ids):
    tok = ids.shape[1]
    match = (ids == 0).astype(F32).astype(BF16)
    count = mm(jnp.ones((ROWS, ids.shape[0]), BF16), match)
    upper = (iota((tok, tok), 0) <= iota((tok, tok), 1)).astype(F32).astype(BF16)
    rank = mm(count.astype(BF16), upper)
    return count > 0.5, (rank + 0.5).astype(jnp.int32) - 1


def move_matrix(transposed):
    big, small = PARTS * 32, NZ * ROWS
    shape = (small, big) if transposed else (big, small)
    a = iota(shape, 1 if transposed else 0)
    b = iota(shape, 0 if transposed else 1)
    p, j, r = a >> 5, (a >> 3) & 3, a & 7
    return ((b == j * ROWS + p * CAP + r) & (r < CAP)).astype(F32).astype(BF16)


def moe_kernel(ids_hbm, gates_hbm, tok_hbm, gate_hbm, up_hbm, down_hbm, out_ref, place_ref, weight_ref,
               ids_v, gates_v, tok, gu, dn, wire, xbuf, ybuf, part, sib_in, y_in, y_out, z_in, z_out,
               loc, ag_recv, ag_z, ag_y, ag_sib,
               s_send, s_recv, y_send, y_recv, z_send, z_recv):
    width = wire.shape[2]
    g, dev, c = lax.axis_index("groups"), lax.axis_index("dev"), lax.axis_index("sub")
    z, y = dev // 2, dev % 2
    others = [(z + j) % NZ for j in (1, 3, 2)]
    y_dev, sib_dev = (g, z * 2 + 1 - y, c), (g, dev, 1 - c)

    barrier = pltpu.get_barrier_semaphore()

    def greet(device):
        pl.semaphore_signal(barrier, inc=1, device_id=device, device_id_type=MESH)

    load_tok = pltpu.make_async_copy(tok_hbm, tok, loc.at[0])
    load_gate = pltpu.make_async_copy(gate_hbm.at[0], gu.at[:, 0:128], loc.at[1])
    load_up = pltpu.make_async_copy(up_hbm.at[0], gu.at[:, 128:256], loc.at[2])
    load_down = pltpu.make_async_copy(down_hbm.at[0], dn, loc.at[3])
    load_ids = pltpu.make_async_copy(ids_hbm, ids_v, loc.at[4])
    load_gates = pltpu.make_async_copy(gates_hbm, gates_v, loc.at[5])
    load_ids.start()
    load_tok.start()
    load_gates.start()
    greet(sib_dev)
    greet(y_dev)
    for zz in others:
        greet((g, zz * 2 + y, c))
    load_gate.start()
    load_up.start()
    load_down.start()

    def remote(src, dst, ss, rs, device):
        return pltpu.make_async_remote_copy(
            src_ref=src, dst_ref=dst, send_sem=ss, recv_sem=rs, device_id=device, device_id_type=MESH)

    def slot(zz, yy, cc):
        return zz * 4 + yy * 2 + cc

    def gather(zz, yy, k, ss, device):
        piece = wire.at[slot(zz, yy, c), pl.ds(k * PIECE, PIECE)]
        return remote(piece, piece, ss, ag_recv.at[slot(zz, yy, c) * NC + k], device)

    def to_z(zz, k):
        return gather(z, y, k, ag_z.at[zz * NC + k], (g, zz * 2 + y, c))

    def to_y(zz, k):
        return gather(zz, y, k, ag_y.at[zz * NC + k], y_dev)

    def to_sib(zz, yy, k):
        return gather(zz, yy, k, ag_sib.at[(zz * 2 + yy) * NC + k], sib_dev)

    def arrived(zz, yy, cc, k):
        piece = wire.at[slot(zz, yy, cc), pl.ds(k * PIECE, PIECE)]
        remote(piece, piece, ag_y.at[0], ag_recv.at[slot(zz, yy, cc) * NC + k], y_dev).wait_recv()

    load_ids.wait()
    count, place = lane_plan(ids_v[...])
    row = iota(place.shape, 0)
    load_tok.wait()
    acc = jnp.zeros((ROWS, width), F32)
    for p in range(PARTS):
        r = row - p * CAP
        sel = (count & (place == r) & (r >= 0) & (r < CAP)).astype(F32).astype(BF16)
        acc += mm(sel, tok[:, p * width:(p + 1) * width])
    wire[slot(z, y, c)] = acc.astype(BF16)

    pl.semaphore_wait(barrier, NZ + 1)

    for k in range(NC):
        for zz in others:
            to_z(zz, k).start()
        to_y(z, k).start()
    for k in range(NC):
        to_sib(z, y, k).start()

    def relay_z(zz, k):
        arrived(zz, y, c, k)
        to_y(zz, k).start()
        to_sib(zz, y, k).start()

    def relay_sib(zz, k):
        arrived(zz, 1 - y, c, k)
        to_sib(zz, 1 - y, k).start()

    load_gates.wait()
    ids, gate_cols = ids_v[...].T, gates_v[...].T
    tokens = ids.shape[0]
    hit = ids == 0
    match = hit.astype(F32)
    weight = jnp.sum(jnp.where(hit, gate_cols, 0.0), axis=1, keepdims=True)
    named = jnp.sum(match, axis=1, keepdims=True) > 0.5
    lower = (iota((tokens, tokens), 0) >= iota((tokens, tokens), 1)).astype(F32).astype(BF16)
    rank = jnp.sum(mm(lower, match.astype(BF16)), axis=1, keepdims=True)
    taken = (rank + 0.5).astype(jnp.int32) - 1
    taken = jnp.where(named & (taken < CAP), taken, -ROWS)
    place_ref[...] = jnp.broadcast_to(taken, place_ref.shape)
    weight_ref[...] = jnp.broadcast_to(weight, weight_ref.shape)

    for k in range(NC):
        for zz in others:
            relay_z(zz, k)
        relay_sib(z, k)
        if k > 0:
            for zz in others:
                relay_sib(zz, k - 1)
    for zz in others:
        relay_sib(zz, NC - 1)

    half = z // 2
    far = NZ - 1 - (NZ - 1) * half
    mid = 2 - half
    order = (far, mid, 6 - far - mid - z, z)

    move = move_matrix(False)
    for zz in order[::-1]:
        for k in range(NC):
            arrived(zz, 0, 1 - c, k)
            arrived(zz, 1, 1 - c, k)
        rows = mm(move, wire[pl.ds(zz * 4, 4)].reshape(4 * ROWS, width)).astype(BF16)
        for p in range(PARTS):
            xbuf[pl.ds(pl.multiple_of(zz * 32, 32), 32), p * width:(p + 1) * width] = rows[p * 32:(p + 1) * 32]

    load_gate.wait()
    load_up.wait()
    act = jnp.zeros((NZ * 32, 256), F32)
    for p in range(PARTS):
        act += mm(xbuf[:, p * width:(p + 1) * width], gu[p * width:(p + 1) * width, :])
    gate, upv = act[:, :128], act[:, 128:]
    hidden = (gate / (1.0 + jnp.exp(-gate)) * upv).astype(BF16)

    load_down.wait()
    for p in range(PARTS):
        val = mm(hidden, dn[:, p * width:(p + 1) * width]).astype(BF16)
        for zz in range(NZ):
            ybuf[zz, p * 32:(p + 1) * 32] = val[zz * 32:(zz + 1) * 32]

    def rows_of(k):
        return pl.ds(k * PIECE, PIECE)

    def s_copy(zz, yy, k):
        n = (zz * 2 + yy) * NC + k
        return remote(part.at[slot(zz, yy, 1 - c), rows_of(k)], sib_in.at[zz * 2 + yy, rows_of(k)],
                      s_send.at[n], s_recv.at[n], sib_dev)

    def line(src, dst, ss, rs, device):
        def copy(zz, k):
            n = zz * NC + k
            return remote(src.at[zz, rows_of(k)], dst.at[zz, rows_of(k)], ss.at[n], rs.at[n], device)
        return copy

    y_copy = line(y_out, y_in, y_send, y_recv, y_dev)

    def z_copy(zz, k):
        return remote(z_out.at[zz, rows_of(k)], z_in.at[z, rows_of(k)],
                      z_send.at[zz * NC + k], z_recv.at[z * NC + k], (g, zz * 2 + y, c))

    def z_arrived(zz, k):
        piece = z_in.at[zz, rows_of(k)]
        remote(piece, piece, z_send.at[0], z_recv.at[zz * NC + k], (g, zz * 2 + y, c)).wait_recv()

    back = move_matrix(True)
    for zz in order:
        vals = mm(back, ybuf[zz]).astype(BF16)
        part[pl.ds(zz * 4, 4)] = vals.reshape(4, ROWS, width)
        for yy in (1 - y, y):
            for k in range(NC):
                s_copy(zz, yy, k).start()

    for zz in order:
        for k in range(NC):
            s_copy(zz, 1 - y, k).wait_recv()
            at = rows_of(k)
            y_out[zz, at] = (part[slot(zz, 1 - y, c), at].astype(F32) + sib_in[zz * 2 + 1 - y, at].astype(F32)).astype(BF16)
            y_copy(zz, k).start()

    def mine(zz, k):
        s_copy(zz, y, k).wait_recv()
        y_copy(zz, k).wait_recv()
        at = rows_of(k)
        return part[slot(zz, y, c), at].astype(F32) + sib_in[zz * 2 + y, at].astype(F32) + y_in[zz, at].astype(F32)

    for zz in order[:3]:
        for k in range(NC):
            z_out[zz, rows_of(k)] = mine(zz, k).astype(BF16)
            z_copy(zz, k).start()
    for k in range(NC):
        total = mine(z, k)
        for zz in others:
            z_arrived(zz, k)
            total += z_in[zz, rows_of(k)].astype(F32)
        out_ref[rows_of(k)] = total

    for k in range(NC):
        for zz in others:
            to_z(zz, k).wait_send()
            z_copy(zz, k).wait_send()
        for zz in range(NZ):
            to_y(zz, k).wait_send()
            y_copy(zz, k).wait_send()
            for yy in range(2):
                to_sib(zz, yy, k).wait_send()
                s_copy(zz, yy, k).wait_send()


def spread_kernel(place_hbm, weight_hbm, merged_hbm, out_hbm, place_ref, weight_ref, merged_ref, stage, sems):
    loads = [pltpu.make_async_copy(src, dst, sems.at[PARTS + i]) for i, (src, dst) in enumerate(
        ((place_hbm, place_ref), (weight_hbm, weight_ref), (merged_hbm, merged_ref)))]
    for load in loads:
        load.start()
    for load in loads:
        load.wait()
    tok, width = place_ref.shape[0], merged_ref.shape[1]
    place, weight = place_ref[:, :ROWS], weight_ref[:, :1]
    merged = merged_ref[...]
    high = merged.astype(BF16)
    rest = merged - high.astype(F32)
    middle = rest.astype(BF16)
    low = (rest - middle.astype(F32)).astype(BF16)
    col = iota((tok, ROWS), 1)
    copies = []
    for p in range(PARTS):
        sel = (place == col - p * CAP).astype(F32).astype(BF16)
        val = (mm(sel, high) + mm(sel, middle)) + mm(sel, low)
        stage[:, p * width:(p + 1) * width] = (val * weight).astype(BF16)
        cols = pl.ds(p * width, width)
        copy = pltpu.make_async_copy(stage.at[:, cols], out_hbm.at[:, cols], sems.at[p])
        copy.start()
        copies.append(copy)
    for copy in copies:
        copy.wait()


def fast(tokens, expert_ids, gate_values, gate_proj, up_proj, down_proj):
    tok, model = tokens.shape
    width = model // PARTS
    ids, gates = expert_ids.T, gate_values.T
    vmem = pl.BlockSpec(memory_space=pltpu.VMEM)
    hbm = pl.BlockSpec(memory_space=pltpu.HBM)
    dma = pltpu.SemaphoreType.DMA

    def blocks(n):
        return pltpu.VMEM((n, ROWS, width), BF16)

    merged, place, weight = pl.pallas_call(
        moe_kernel,
        out_shape=(jax.ShapeDtypeStruct((ROWS, width), F32), jax.ShapeDtypeStruct((tok, 128), jnp.int32),
                   jax.ShapeDtypeStruct((tok, 128), F32)),
        in_specs=[hbm] * 6,
        out_specs=(vmem, vmem, vmem),
        scratch_shapes=[
            pltpu.VMEM(ids.shape, jnp.int32),
            pltpu.VMEM(gates.shape, F32),
            pltpu.VMEM((tok, model), BF16),
            pltpu.VMEM((model, 256), BF16),
            pltpu.VMEM((128, model), BF16),
            blocks(SH),
            pltpu.VMEM((NZ * 32, model), BF16),
            pltpu.VMEM((NZ, PARTS * 32, width), BF16),
            blocks(SH), blocks(8), blocks(NZ), blocks(NZ), blocks(NZ), blocks(NZ),
            dma((6,)), dma((SH * NC,)), dma((NZ * NC,)), dma((NZ * NC,)), dma((8 * NC,)),
            dma((8 * NC,)), dma((8 * NC,)), dma((NZ * NC,)), dma((NZ * NC,)), dma((NZ * NC,)), dma((NZ * NC,)),
        ],
        compiler_params=pltpu.CompilerParams(
            collective_id=0, has_side_effects=True, vmem_limit_bytes=60 * 1024 * 1024),
        name="expert",
    )(ids, gates, tokens, gate_proj, up_proj, down_proj)
    return pl.pallas_call(
        spread_kernel,
        out_shape=jax.ShapeDtypeStruct((tok, model), BF16),
        in_specs=[hbm, hbm, hbm],
        out_specs=hbm,
        scratch_shapes=[pltpu.VMEM(place.shape, jnp.int32), pltpu.VMEM(weight.shape, F32), pltpu.VMEM(merged.shape, F32),
                        pltpu.VMEM((tok, model), BF16), dma((PARTS + 3,))],
        compiler_params=pltpu.CompilerParams(vmem_limit_bytes=60 * 1024 * 1024),
        name="spread",
    )(place, weight, merged)


def plan(expert_ids, gate_values, window):
    experts = jnp.arange(window, dtype=jnp.int32)
    matches = expert_ids[:, :, None] == experts[None, None, :]
    counts = jnp.sum(matches.astype(jnp.int32), axis=1)
    weight = jnp.sum(
        jnp.where(matches, gate_values[:, :, None], jnp.zeros_like(gate_values[:, :, None])), axis=1
    )
    ranking = jnp.cumsum(counts, axis=0) - 1
    slot_ids = jnp.arange(CAP, dtype=jnp.int32)
    chosen = (counts.T[:, None, :] == 1) & (ranking.T[:, None, :] == slot_ids[None, :, None])
    return (chosen, weight)


def general(tokens, expert_ids, gate_values, gate_proj, up_proj, down_proj):
    devices = lax.axis_size("dev") * lax.axis_size("sub")
    window = devices // SH
    model_width = tokens.shape[1]
    chosen, weight = plan(expert_ids, gate_values, window)
    picked = chosen.astype(jnp.bfloat16).reshape(window * CAP, tokens.shape[0])
    outbound = jnp.dot(picked, tokens, preferred_element_type=jnp.float32).astype(jnp.bfloat16)
    outbound = outbound.reshape(window, 1, CAP, model_width)
    sendbuf = jnp.broadcast_to(outbound, (window, SH, CAP, model_width)).reshape(
        devices, CAP, model_width
    )
    arrived = lax.all_to_all(sendbuf, ("dev", "sub"), split_axis=0, concat_axis=0, tiled=True)
    row_block = arrived.reshape(devices * CAP, model_width)
    gate_act = jnp.dot(row_block, gate_proj[0], preferred_element_type=jnp.float32)
    up_act = jnp.dot(row_block, up_proj[0], preferred_element_type=jnp.float32)
    hidden = (jax.nn.silu(gate_act) * up_act).astype(jnp.bfloat16)
    partial_value = jnp.dot(hidden, down_proj[0], preferred_element_type=jnp.float32).astype(
        jnp.bfloat16
    )
    returned = lax.all_to_all(
        partial_value.reshape(devices, CAP, model_width),
        ("dev", "sub"),
        split_axis=0,
        concat_axis=0,
        tiled=True,
    )
    merged = jnp.sum(returned.reshape(window, SH, CAP, model_width).astype(jnp.float32), axis=1)
    combine = (chosen.astype(jnp.float32) * weight.T[:, None, :]).reshape(
        window * CAP, tokens.shape[0]
    )
    moe_out = jnp.dot(
        combine.T,
        merged.reshape(window * CAP, model_width),
        precision=lax.Precision.HIGHEST,
        preferred_element_type=jnp.float32,
    )
    return moe_out.astype(jnp.bfloat16)


def solution(mesh):
    placed = (
        P(("groups", "dev", "sub"), None),
        P(("groups", "dev", "sub"), None),
        P(("groups", "dev", "sub"), None),
        P(("dev", "sub"), None, None),
        P(("dev", "sub"), None, None),
        P(("dev", "sub"), None, None),
    )
    one_expert = mesh.shape["dev"] == 2 * NZ and mesh.shape["sub"] == 2
    return jax.shard_map(
        fast if one_expert else general,
        mesh=mesh,
        in_specs=placed,
        out_specs=P(("groups", "dev", "sub"), None),
        check_vma=False,
    )
```
